32 devices in a mesh: view: 8 (over z, x), tile: 4 (over y, core).
Axes of the slice: x: 2, y: 2, z: 4, core: 2. Of those that a mesh axis runs over, the one named last changes fastest.
Arguments:
- ref_feat: bfloat16 [32, 8192], P(None, 'tile'), may hold values from -6 to 6
- src_feat: bfloat16 [8, 4, 32, 6144], P('view', 'tile'), may hold values from -6 to 6
- taps: int32 [8, 128, 4], P('view', None, 'tile'), may hold values from 0 to 3838, as said below
- weights: bfloat16 [8, 128, 4, 8192], P('view', None, None, 'tile'), may hold values from 0 to 1, as said below
- conv_weight: float32 [3, 3, 3, 8], replicated, may hold values from -0.4375 to 0.4375
Outputs:
- log_prob: float32 [128, 8192], P('view', 'tile')
- depth_map: float32 [8192], P('tile')
The draws below stay inside these ranges and needn't reach their ends.
Inputs may be any that keep to these rules, and one draw needn't show every extreme that they name: Every offset keeps all four taps of every pixel of the band inside the band's window. For each view, plane and pixel the four weights are (1 - a)(1 - b), a(1 - b), (1 - a) b, a b for some a, b in 0 to 1, rounded to bfloat16.
All inputs are finite; a program needn't handle non-finite values.
Results may differ from the reference program's by a relative error of at most 0.0003.
Values sent between devices are 32-bit elements; how exact they have to be, the bound alone decides.
A program may use at most 128 MiB of HBM per device.

```python
import jax
import jax.numpy as jnp
from jax import lax

C = 32
G = 8
D = 128
ROWS = 8
COLS = 256
SRC_ROWS = 24
Q = 6144
VIEWS = 8
TILES = 4
PIX = 8192


def draw_taps(key, part):
    keys = jax.random.split(key, 3)
    top_offset = (SRC_ROWS - ROWS - 1) * COLS - 2
    row_shift = jax.random.randint(keys[0], (VIEWS, D, TILES), 0, SRC_ROWS - ROWS - 1)
    disparity = jax.random.randint(keys[1], (VIEWS, 1, 1), 0, COLS // 2)
    col_shift = jnp.arange(D, dtype=jnp.int32)[None, :, None] * disparity // D + jax.random.randint(keys[2], (VIEWS, D, TILES), 0, COLS // 2)
    offset = jnp.clip(row_shift * COLS + col_shift, 0, top_offset).astype(jnp.int32)
    offset = offset.at[0, 0, 0].set(top_offset)
    offset = offset.at[0, 1, 0].set(0)
    return offset


def draw_weights(key, part):
    keys = jax.random.split(key, 2)
    frac_col = jax.random.uniform(keys[0], (VIEWS, D, 1, PIX), jnp.float32)
    frac_row = jax.random.uniform(keys[1], (VIEWS, D, 1, PIX), jnp.float32)
    stacked = jnp.concatenate([(1.0 - frac_col) * (1.0 - frac_row), frac_col * (1.0 - frac_row), (1.0 - frac_col) * frac_row, frac_col * frac_row], axis=2)
    return stacked.astype(jnp.bfloat16)


def level_of(stream_key, dims, cuts, smallest, largest):
    loudness, own = 1.0, jax.random.fold_in(stream_key, 6)
    for axis_at, shards_of in cuts:
        heights = jnp.exp(jax.random.uniform(jax.random.fold_in(own, axis_at), (shards_of,), jnp.float32, smallest / len(cuts), largest / len(cuts)))
        loudness = loudness * jnp.repeat(heights, dims[axis_at] // shards_of).reshape([-1 if axis == axis_at else 1 for axis in range(len(dims))])
    return loudness


def noise(rng, extent, width, limit, pieces=(), held_as=jnp.bfloat16):
    array = width * jax.random.normal(rng, extent, jnp.float32)
    if pieces:
        array = array * level_of(rng, extent, pieces, -0.22, 0.18)
    return jnp.clip(array, -limit, limit).astype(held_as)


def setup_inputs(seed: int = 0) -> dict:
    splits = jax.random.split(jax.random.key(seed), 6)
    return {
        "ref_feat": noise(splits[0], (C, PIX), 1.0, 6.0, ((1, 4),)),
        "src_feat": noise(splits[1], (VIEWS, TILES, C, Q), 1.0, 6.0, ((0, 8), (1, 4))),
        "taps": draw_taps(jax.random.fold_in(splits[5], 71), 0),
        "weights": draw_weights(jax.random.fold_in(splits[5], 71), 0),
        "conv_weight": noise(splits[4], (3, 3, 3, G), (27 * G) ** -0.5, 0.4375, (), jnp.float32),
    }


def correlate_plane(window, ref_values, offset, plane_weights, group_count, col_count):
    pixel_count = ref_values.shape[1]
    chan_count = ref_values.shape[0]
    warped = jnp.zeros((chan_count, pixel_count), jnp.float32)
    shifts = (0, 1, col_count, col_count + 1)
    for tap_index in range(4):
        start = (offset + shifts[tap_index]).astype(jnp.int32)
        cut = lax.dynamic_slice_in_dim(window, start, pixel_count, 1).astype(jnp.float32)
        warped = warped + plane_weights[tap_index].astype(jnp.float32)[None, :] * cut
    products = (ref_values * warped).reshape(group_count, chan_count // group_count, pixel_count)
    return jnp.sum(products, axis=1) / (chan_count // group_count)


def stencil(extended, kernel, depth_count, row_count, col_count):
    result = jnp.zeros((depth_count, row_count, col_count), jnp.float32)
    for shift_d in range(3):
        for shift_r in range(3):
            for shift_c in range(3):
                window_cut = extended[shift_d:shift_d + depth_count, :, shift_r:shift_r + row_count, shift_c:shift_c + col_count]
                result = result + jnp.sum(window_cut * kernel[shift_d, shift_r, shift_c][None, :, None, None], axis=1)
    return result


def reference(ref_feat, src_feat, taps, weights, conv_weight):
    band_pixels = ROWS * COLS
    ref_bands = jnp.transpose(ref_feat.astype(jnp.float32).reshape(C, TILES, band_pixels), (1, 0, 2))

    def view_step(cost_volume, inputs_view):
        source_view, taps_view, weights_view = inputs_view
        weight_bands = weights_view.reshape(D, 4, TILES, band_pixels)

        def plane_step(plane_inputs):
            plane_offsets, plane_weights = plane_inputs
            per_band = jax.vmap(lambda window, ref_band, offset, band_weights: correlate_plane(window, ref_band, offset, band_weights, G, COLS), in_axes=(0, 0, 0, 1))(source_view, ref_bands, plane_offsets, plane_weights)
            return jnp.transpose(per_band, (1, 0, 2)).reshape(G, PIX)

        corr_view = lax.map(plane_step, (taps_view, weight_bands))
        return cost_volume + corr_view, None

    cost_volume, _ = lax.scan(view_step, jnp.zeros((D, G, PIX), jnp.float32), (src_feat, taps, weights))
    row_all = PIX // COLS
    extended = jnp.pad(cost_volume.reshape(D, G, row_all, COLS), ((1, 1), (0, 0), (1, 1), (1, 1)))
    filtered = stencil(extended, conv_weight, D, row_all, COLS)
    logit_value = 4.0 * jnp.tanh(0.5 * filtered)
    exp_values = jnp.exp(logit_value)
    plane_value = jnp.arange(D, dtype=jnp.float32) / (D - 1)
    exp_total = jnp.sum(exp_values, axis=0)
    log_prob = (logit_value - jnp.log(exp_total)[None]).reshape(D, PIX)
    depth_map = (jnp.sum(exp_values * plane_value[:, None, None], axis=0) / exp_total).reshape(PIX)
    return log_prob, depth_map
```

```python
import functools

import jax
import jax.numpy as jnp
from jax import lax
from jax.experimental import pallas as pl
from jax.experimental.pallas import tpu as pltpu
from jax.sharding import PartitionSpec as P

COLS = 256
LANES = 128


def split_bf16(x):
    hi = x.astype(jnp.bfloat16)
    lo = (x - hi.astype(jnp.float32)).astype(jnp.bfloat16)
    return hi, lo


def dot32(a, b):
    return lax.dot_general(a, b, (((1,), (0,)), ((), ())), preferred_element_type=jnp.float32)


def load_features(src_ref, ref_ref, stage, win, ref_f, groups):
    chans = ref_ref.shape[0]
    per_group = chans // groups
    for source, scale, target in ((src_ref.at[0, 0], 1.0, win), (ref_ref, 1.0 / per_group, ref_f)):
        for t in range(target.shape[0]):
            cut = source[:, t * LANES : (t + 1) * LANES].astype(jnp.float32)
            stage[t * chans : (t + 1) * chans] = cut * scale
        for t in range(target.shape[0]):
            for c in range(per_group):
                target[t, c * groups : (c + 1) * groups] = stage[
                    pl.ds(t * chans + c, groups, stride=per_group), :
                ]


def correlate_pair(pair, taps_ref, weights_ref, win, ref_f, wbuf, chi, clo, groups):
    tiles = ref_f.shape[0]
    chans = ref_f.shape[1]
    step = COLS // LANES
    lane = lax.broadcasted_iota(jnp.int32, (chans, LANES), 1)
    for k in range(2):
        wbuf[k] = weights_ref[0, 2 * pair + k].astype(jnp.float32)
    planes = []
    for k in range(2):
        offset = taps_ref[2 * pair + k]
        first = offset >> 7
        rest = offset & (LANES - 1)
        planes.append((first, (LANES - rest) & (LANES - 1), LANES - 1 - rest, lane < LANES - rest, lane < LANES - 1 - rest))
    results = []
    for k in range(2):
        first, turn0, turn1, mask0, mask1 = planes[k]
        cuts = []
        before = None
        out = []
        for j in range(tiles + step + 1):
            raw = win[first + j]
            turned = (pltpu.roll(raw, turn0, 1), pltpu.roll(raw, turn1, 1))
            if before is not None:
                cuts.append((jnp.where(mask0, before[0], turned[0]), jnp.where(mask1, before[1], turned[1])))
            before = turned
            i = len(cuts) - 1 - step
            if i >= 0:
                lanes = slice(i * LANES, (i + 1) * LANES)
                taps4 = (cuts[i][0], cuts[i][1], cuts[i + step][0], cuts[i + step][1])
                warped = None
                for tap in range(4):
                    row = jnp.broadcast_to(wbuf[k, tap : tap + 1, lanes], (groups, LANES))
                    row = jnp.concatenate([row] * (chans // groups), axis=0)
                    warped = row * taps4[tap] if warped is None else warped + row * taps4[tap]
                product = warped * ref_f[i]
                total = product[:groups]
                for c in range(1, chans // groups):
                    total = total + product[c * groups : (c + 1) * groups]
                out.append(total)
        results.append(out)
    start = pl.multiple_of((pair + 1) * 2 * groups, 2 * groups)
    for i in range(tiles):
        hi, lo = split_bf16(jnp.concatenate([results[0][i], results[1][i]], axis=0))
        chi[pl.ds(start, 2 * groups), i * LANES : (i + 1) * LANES] = hi
        clo[pl.ds(start, 2 * groups), i * LANES : (i + 1) * LANES] = lo


def filter_slab(slab, size, groups, whi, wlo, chi, clo):
    pixels = chi.shape[1]
    start = pl.multiple_of(slab * size * groups, 2 * groups)
    high = chi[pl.ds(start, (size + 4) * groups), :]
    low = clo[pl.ds(start, (size + 4) * groups), :]
    part = dot32(whi[...], high) + dot32(whi[...], low) + dot32(wlo[...], high)
    zeros = jnp.zeros((size, COLS), jnp.float32)
    width = pixels + 2 * COLS
    col = lax.broadcasted_iota(jnp.int32, (size, width), 1) & (COLS - 1)
    shifted = []
    for e in range(3):
        total = None
        for b in range(3):
            piece = part[(b * 3 + e) * size : (b * 3 + e + 1) * size]
            pads = [zeros] * (2 - b) + [piece] + [zeros] * b
            piece = jnp.concatenate(pads, axis=1)
            total = piece if total is None else total + piece
        shifted.append(total)
    left = jnp.where(col == 0, 0.0, pltpu.roll(shifted[0], 1, 1))
    right = jnp.where(col == COLS - 1, 0.0, pltpu.roll(shifted[2], width - 1, 1))
    return shifted[1] + left + right


def partial_kernel(size, groups, taps_ref, ref_ref, src_ref, weights_ref, filt_ref, out_ref,
                   stage, win, ref_f, wbuf, chi, clo, whi, wlo):
    planes = weights_ref.shape[1]
    load_features(src_ref, ref_ref, stage, win, ref_f, groups)
    high, low = split_bf16(filt_ref[...])
    whi[...] = high
    wlo[...] = low
    edge = jnp.zeros((2 * groups, chi.shape[1]), jnp.bfloat16)
    for buf in (chi, clo):
        buf[: 2 * groups] = edge
        buf[(planes + 2) * groups :] = edge

    def pair_step(pair, _):
        correlate_pair(pair, taps_ref, weights_ref, win, ref_f, wbuf, chi, clo, groups)
        return 0

    lax.fori_loop(0, planes // 2, pair_step, 0)

    def slab_step(slab, _):
        out_ref[pl.ds(pl.multiple_of(slab * size, size), size), :] = filter_slab(
            slab, size, groups, whi, wlo, chi, clo
        )
        return 0

    lax.fori_loop(0, planes // size, slab_step, 0)


def filter_matrix(conv_weight, size):
    groups = conv_weight.shape[3]
    plane_out = lax.broadcasted_iota(jnp.int32, (size, size + 4), 0)
    plane_in = lax.broadcasted_iota(jnp.int32, (size, size + 4), 1)
    total = 0.0
    for a in range(3):
        band = (plane_in == plane_out + 1 + a)[None, None, :, :, None]
        total = total + jnp.where(band, conv_weight[a][:, :, None, None, :], 0.0)
    return total.reshape(9 * size, (size + 4) * groups)


def partial_scratch(chans, window, pixels, planes, groups, size):
    return [
        pltpu.VMEM((window // LANES * chans, LANES), jnp.float32),
        pltpu.VMEM((window // LANES, chans, LANES), jnp.float32),
        pltpu.VMEM((pixels // LANES, chans, LANES), jnp.float32),
        pltpu.VMEM((2, 4, pixels), jnp.float32),
        pltpu.VMEM(((planes + 4) * groups, pixels), jnp.bfloat16),
        pltpu.VMEM(((planes + 4) * groups, pixels), jnp.bfloat16),
        pltpu.VMEM((9 * size, (size + 4) * groups), jnp.bfloat16),
        pltpu.VMEM((9 * size, (size + 4) * groups), jnp.bfloat16),
    ]


def on_device(ref_feat, src_feat, taps, weights, conv_weight):
    view_count = lax.axis_size("view")
    tile_count = lax.axis_size("tile")
    chans, pixels = ref_feat.shape
    planes = taps.shape[1]
    size = planes // view_count
    groups = conv_weight.shape[3]
    window = src_feat.shape[3]
    rows = pixels // COLS
    vmem = pl.BlockSpec(memory_space=pltpu.VMEM)
    part = pl.pallas_call(
        functools.partial(partial_kernel, size, groups),
        out_shape=jax.ShapeDtypeStruct((planes, pixels + 2 * COLS), jnp.float32),
        in_specs=[pl.BlockSpec(memory_space=pltpu.SMEM), vmem, vmem, vmem, vmem],
        out_specs=vmem,
        scratch_shapes=partial_scratch(chans, window, pixels, planes, groups, size),
        compiler_params=pltpu.CompilerParams(vmem_limit_bytes=48 * 1024 * 1024),
    )(taps[0, :, 0], ref_feat, src_feat, weights, filter_matrix(conv_weight, size))
    slab = lax.psum_scatter(part, "view", scatter_dimension=0, tiled=True)
    up = [(i, i + 1) for i in range(tile_count - 1)]
    down = [(j, i) for i, j in up]
    from_above = lax.ppermute(slab[:, pixels + COLS :], "tile", up)
    from_below = lax.ppermute(slab[:, :COLS], "tile", down)
    z = slab[:, COLS : pixels + COLS]
    z = jnp.concatenate(
        [z[:, :COLS] + from_above, z[:, COLS:-COLS], z[:, -COLS:] + from_below], axis=1
    )
    logit = 4.0 * jnp.tanh(0.5 * z)
    exps = jnp.exp(logit)
    plane = lax.axis_index("view") * size + lax.iota(jnp.int32, size)
    value = plane.astype(jnp.float32) / (planes - 1)
    sums = jnp.stack([jnp.sum(exps, axis=0), jnp.sum(exps * value[:, None], axis=0)])
    sums = lax.psum(sums, "view")
    return logit - jnp.log(sums[0])[None], sums[1] / sums[0]


def solution(mesh):
    placed = (
        P(None, "tile"),
        P("view", "tile", None, None),
        P("view", None, "tile"),
        P("view", None, None, "tile"),
        P(),
    )
    return jax.shard_map(
        on_device,
        mesh=mesh,
        in_specs=placed,
        out_specs=(P("view", "tile"), P("tile")),
        check_vma=False,
    )
```

```python
import functools

import jax
import jax.numpy as jnp
from jax import lax
from jax.experimental import pallas as pl
from jax.experimental.pallas import tpu as pltpu
from jax.sharding import PartitionSpec as P

COLS = 256
LANES = 128
MESH = pl.DeviceIdType.MESH


def split_bf16(x):
    hi = x.astype(jnp.bfloat16)
    lo = (x - hi.astype(jnp.float32)).astype(jnp.bfloat16)
    return hi, lo


def dot32(a, b):
    return lax.dot_general(a, b, (((1,), (0,)), ((), ())), preferred_element_type=jnp.float32)


def load_features(src_ref, ref_ref, stage, win, ref_f, groups):
    chans = ref_ref.shape[0]
    per_group = chans // groups
    for source, scale, target in ((src_ref.at[0, 0], 1.0, win), (ref_ref, 1.0 / per_group, ref_f)):
        for t in range(target.shape[0]):
            cut = source[:, t * LANES : (t + 1) * LANES].astype(jnp.float32)
            stage[t * chans : (t + 1) * chans] = cut * scale
        for t in range(target.shape[0]):
            for c in range(per_group):
                target[t, c * groups : (c + 1) * groups] = stage[
                    pl.ds(t * chans + c, groups, stride=per_group), :
                ]


def correlate_pair(pair, taps_ref, weights_ref, win, ref_f, wbuf, chi, clo, groups):
    tiles = ref_f.shape[0]
    chans = ref_f.shape[1]
    step = COLS // LANES
    lane = lax.broadcasted_iota(jnp.int32, (chans, LANES), 1)
    for k in range(2):
        wbuf[k] = weights_ref[0, 2 * pair + k].astype(jnp.float32)
    planes = []
    for k in range(2):
        offset = taps_ref[2 * pair + k]
        first = offset >> 7
        rest = offset & (LANES - 1)
        planes.append((first, (LANES - rest) & (LANES - 1), LANES - 1 - rest, lane < LANES - rest, lane < LANES - 1 - rest))
    results = []
    for k in range(2):
        first, turn0, turn1, mask0, mask1 = planes[k]
        cuts = []
        before = None
        out = []
        for j in range(tiles + step + 1):
            raw = win[first + j]
            turned = (pltpu.roll(raw, turn0, 1), pltpu.roll(raw, turn1, 1))
            if before is not None:
                cuts.append((jnp.where(mask0, before[0], turned[0]), jnp.where(mask1, before[1], turned[1])))
            before = turned
            i = len(cuts) - 1 - step
            if i >= 0:
                lanes = slice(i * LANES, (i + 1) * LANES)
                taps4 = (cuts[i][0], cuts[i][1], cuts[i + step][0], cuts[i + step][1])
                warped = None
                for tap in range(4):
                    row = jnp.broadcast_to(wbuf[k, tap : tap + 1, lanes], (groups, LANES))
                    row = jnp.concatenate([row] * (chans // groups), axis=0)
                    warped = row * taps4[tap] if warped is None else warped + row * taps4[tap]
                product = warped * ref_f[i]
                total = product[:groups]
                for c in range(1, chans // groups):
                    total = total + product[c * groups : (c + 1) * groups]
                out.append(total)
        results.append(out)
    start = pl.multiple_of((pair + 1) * 2 * groups, 2 * groups)
    for i in range(tiles):
        hi, lo = split_bf16(jnp.concatenate([results[0][i], results[1][i]], axis=0))
        chi[pl.ds(start, 2 * groups), i * LANES : (i + 1) * LANES] = hi
        clo[pl.ds(start, 2 * groups), i * LANES : (i + 1) * LANES] = lo


def filter_slab(slab, size, groups, whi, wlo, chi, clo):
    pixels = chi.shape[1]
    start = pl.multiple_of(slab * size * groups, 2 * groups)
    high = chi[pl.ds(start, (size + 4) * groups), :]
    low = clo[pl.ds(start, (size + 4) * groups), :]
    part = dot32(whi[...], high) + dot32(whi[...], low) + dot32(wlo[...], high)
    zeros = jnp.zeros((size, COLS), jnp.float32)
    width = pixels + 2 * COLS
    col = lax.broadcasted_iota(jnp.int32, (size, width), 1) & (COLS - 1)
    shifted = []
    for e in range(3):
        total = None
        for b in range(3):
            piece = part[(b * 3 + e) * size : (b * 3 + e + 1) * size]
            pads = [zeros] * (2 - b) + [piece] + [zeros] * b
            piece = jnp.concatenate(pads, axis=1)
            total = piece if total is None else total + piece
        shifted.append(total)
    left = jnp.where(col == 0, 0.0, pltpu.roll(shifted[0], 1, 1))
    right = jnp.where(col == COLS - 1, 0.0, pltpu.roll(shifted[2], width - 1, 1))
    return shifted[1] + left + right


def peer_at(view, tile):
    return {"view": view, "tile": tile}


def greet_peers(views, tiles, barrier):
    view, tile = lax.axis_index("view"), lax.axis_index("tile")
    for k in range(1, views):
        pl.semaphore_signal(barrier, inc=1, device_id=peer_at(lax.rem(view + k, views), tile), device_id_type=MESH)
    for k in (1, tiles - 1):
        pl.semaphore_signal(barrier, inc=1, device_id=peer_at(view, lax.rem(tile + k, tiles)), device_id_type=MESH)


def finish(views, tiles, zown, zin, hout, hin, sout, sin, slab_wait, hsend, hrecv, ssend, srecv, prob_ref, depth_ref):
    view, tile = lax.axis_index("view"), lax.axis_index("tile")
    size, width = zown.shape
    total = zown[...]
    for k in range(views - 1):
        slab_wait(k)
        total = total + zin[k]
    hout[0] = total[:, :COLS]
    hout[1] = total[:, width - COLS :]
    halo = []
    for side, k in ((0, tiles - 1), (1, 1)):
        halo.append(pltpu.make_async_remote_copy(
            src_ref=hout.at[side], dst_ref=hin.at[side], send_sem=hsend.at[side], recv_sem=hrecv.at[side],
            device_id=peer_at(view, lax.rem(tile + k, tiles)), device_id_type=MESH))
    for copy in halo:
        copy.start()
    for copy in halo:
        copy.wait()
    below = jnp.where(tile < tiles - 1, hin[0], 0.0)
    above = jnp.where(tile > 0, hin[1], 0.0)
    z = total[:, COLS : width - COLS]
    z = jnp.concatenate([z[:, :COLS] + above, z[:, COLS:-COLS], z[:, -COLS:] + below], axis=1)
    logit = 4.0 * jnp.tanh(0.5 * z)
    exps = jnp.exp(logit)
    plane = view * size + lax.broadcasted_iota(jnp.int32, exps.shape, 0)
    value = plane.astype(jnp.float32) / (size * views - 1)
    sout[0:1] = jnp.sum(exps, axis=0, keepdims=True)
    sout[1:2] = jnp.sum(exps * value, axis=0, keepdims=True)
    sums = []
    for k in range(views - 1):
        sums.append(pltpu.make_async_remote_copy(
            src_ref=sout, dst_ref=sin.at[k], send_sem=ssend.at[k], recv_sem=srecv.at[k],
            device_id=peer_at(lax.rem(view + 1 + k, views), tile), device_id_type=MESH))
    for copy in sums:
        copy.start()
    both = sout[...]
    for k, copy in enumerate(sums):
        copy.wait_recv()
        both = both + sin[k]
    prob_ref[...] = logit - jnp.log(both[0:1])
    depth_ref[...] = both[1:2] / both[0:1]
    for copy in sums:
        copy.wait_send()


def slab_copy(views, k, source, zin, zsend, zrecv):
    view, tile = lax.axis_index("view"), lax.axis_index("tile")
    return pltpu.make_async_remote_copy(
        src_ref=source, dst_ref=zin.at[k], send_sem=zsend.at[k], recv_sem=zrecv.at[k],
        device_id=peer_at(lax.rem(view + 1 + k, views), tile), device_id_type=MESH)


def prepare(taps_ref, ref_ref, src_ref, filt_ref, stage, win, ref_f, chi, clo, whi, wlo, groups):
    load_features(src_ref, ref_ref, stage, win, ref_f, groups)
    high, low = split_bf16(filt_ref[...])
    whi[...] = high
    wlo[...] = low
    edge = jnp.zeros((2 * groups, chi.shape[1]), jnp.bfloat16)
    for buf in (chi, clo):
        buf[: 2 * groups] = edge
        buf[chi.shape[0] - 2 * groups :] = edge


def whole_kernel(size, groups, views, tiles, taps_ref, ref_ref, src_ref, weights_ref, filt_ref, prob_ref, depth_ref,
                 stage, win, ref_f, wbuf, chi, clo, whi, wlo, zout,
                 zin, hout, hin, sout, sin, zsend, zrecv, hsend, hrecv, ssend, srecv):
    barrier = pltpu.get_barrier_semaphore()
    greet_peers(views, tiles, barrier)
    prepare(taps_ref, ref_ref, src_ref, filt_ref, stage, win, ref_f, chi, clo, whi, wlo, groups)
    pl.semaphore_wait(barrier, views + 1)
    view = lax.axis_index("view")
    pairs = weights_ref.shape[1] // 2
    half = size // 2

    def pair_step(q, _):
        pair = lax.rem(half * (view + 1) - 1 + q, pairs)
        correlate_pair(pair, taps_ref, weights_ref, win, ref_f, wbuf, chi, clo, groups)
        return 0

    def slab_step(k, _):
        first = half * k + jnp.where(k > 0, 2, 0)
        last = half * (k + 1) + jnp.where(k < views - 1, 2, 1)
        lax.fori_loop(first, last, pair_step, 0)
        slab = lax.rem(view + 1 + k, views)
        zout[k] = filter_slab(slab, size, groups, whi, wlo, chi, clo)

        @pl.when(k < views - 1)
        def _():
            slab_copy(views, k, zout.at[k], zin, zsend, zrecv).start()

        return 0

    lax.fori_loop(0, views, slab_step, 0)
    copies = [slab_copy(views, k, zout.at[k], zin, zsend, zrecv) for k in range(views - 1)]
    finish(views, tiles, zout.at[views - 1], zin, hout, hin, sout, sin,
           lambda k: copies[k].wait_recv(), hsend, hrecv, ssend, srecv, prob_ref, depth_ref)
    for copy in copies:
        copy.wait_send()


def filter_matrix(conv_weight, size):
    groups = conv_weight.shape[3]
    plane_out = lax.broadcasted_iota(jnp.int32, (size, size + 4), 0)
    plane_in = lax.broadcasted_iota(jnp.int32, (size, size + 4), 1)
    total = 0.0
    for a in range(3):
        band = (plane_in == plane_out + 1 + a)[None, None, :, :, None]
        total = total + jnp.where(band, conv_weight[a][:, :, None, None, :], 0.0)
    return total.reshape(9 * size, (size + 4) * groups)


def partial_scratch(chans, window, pixels, planes, groups, size):
    return [
        pltpu.VMEM((window // LANES * chans, LANES), jnp.float32),
        pltpu.VMEM((window // LANES, chans, LANES), jnp.float32),
        pltpu.VMEM((pixels // LANES, chans, LANES), jnp.float32),
        pltpu.VMEM((2, 4, pixels), jnp.float32),
        pltpu.VMEM(((planes + 4) * groups, pixels), jnp.bfloat16),
        pltpu.VMEM(((planes + 4) * groups, pixels), jnp.bfloat16),
        pltpu.VMEM((9 * size, (size + 4) * groups), jnp.bfloat16),
        pltpu.VMEM((9 * size, (size + 4) * groups), jnp.bfloat16),
    ]


def exchange_scratch(views, size, pixels):
    width = pixels + 2 * COLS
    return [
        pltpu.VMEM((views - 1, size, width), jnp.float32),
        pltpu.VMEM((2, size, COLS), jnp.float32),
        pltpu.VMEM((2, size, COLS), jnp.float32),
        pltpu.VMEM((2, pixels), jnp.float32),
        pltpu.VMEM((views - 1, 2, pixels), jnp.float32),
        pltpu.SemaphoreType.DMA((views - 1,)),
        pltpu.SemaphoreType.DMA((views - 1,)),
        pltpu.SemaphoreType.DMA((2,)),
        pltpu.SemaphoreType.DMA((2,)),
        pltpu.SemaphoreType.DMA((views - 1,)),
        pltpu.SemaphoreType.DMA((views - 1,)),
    ]


def on_device(ref_feat, src_feat, taps, weights, conv_weight):
    views = lax.axis_size("view")
    tiles = lax.axis_size("tile")
    chans, pixels = ref_feat.shape
    planes = taps.shape[1]
    size = planes // views
    groups = conv_weight.shape[3]
    window = src_feat.shape[3]
    width = pixels + 2 * COLS
    vmem = pl.BlockSpec(memory_space=pltpu.VMEM)
    inputs = (taps[0, :, 0], ref_feat, src_feat, weights, filter_matrix(conv_weight, size))
    in_specs = [pl.BlockSpec(memory_space=pltpu.SMEM), vmem, vmem, vmem, vmem]
    outs = (jax.ShapeDtypeStruct((size, pixels), jnp.float32), jax.ShapeDtypeStruct((1, pixels), jnp.float32))
    local = partial_scratch(chans, window, pixels, planes, groups, size)
    log_prob, depth_map = pl.pallas_call(
        functools.partial(whole_kernel, size, groups, views, tiles),
        out_shape=outs,
        in_specs=in_specs,
        out_specs=(vmem, vmem),
        scratch_shapes=local + [pltpu.VMEM((views, size, width), jnp.float32)] + exchange_scratch(views, size, pixels),
        compiler_params=pltpu.CompilerParams(collective_id=0, has_side_effects=True, vmem_limit_bytes=48 * 1024 * 1024),
    )(*inputs)
    return log_prob, depth_map[0]


def solution(mesh):
    placed = (
        P(None, "tile"),
        P("view", "tile", None, None),
        P("view", None, "tile"),
        P("view", None, None, "tile"),
        P(),
    )
    return jax.shard_map(
        on_device,
        mesh=mesh,
        in_specs=placed,
        out_specs=(P("view", "tile"), P("tile")),
        check_vma=False,
    )
```

```python
import functools

import jax
import jax.numpy as jnp
from jax import lax
from jax.experimental import pallas as pl
from jax.experimental.pallas import tpu as pltpu
from jax.sharding import PartitionSpec as P

COLS = 256
LANES = 128
MESH = pl.DeviceIdType.MESH


def split_bf16(x):
    hi = x.astype(jnp.bfloat16)
    lo = (x - hi.astype(jnp.float32)).astype(jnp.bfloat16)
    return hi, lo


def dot32(a, b):
    return lax.dot_general(a, b, (((1,), (0,)), ((), ())), preferred_element_type=jnp.float32)


def load_features(src_ref, ref_ref, stage, win, ref_f, shift, groups):
    chans = ref_ref.shape[0]
    per_group = chans // groups

    def ordered(source, scale, t):
        cut = source[:, t * LANES : (t + 1) * LANES].astype(jnp.float32)
        stage[t * chans : (t + 1) * chans] = cut * scale
        return jnp.concatenate(
            [stage[pl.ds(t * chans + c, groups, stride=per_group), :] for c in range(per_group)], axis=0
        )

    for t in range(win.shape[0] + 1):
        tile = ordered(src_ref.at[0, 0], 1.0, t).astype(jnp.bfloat16)
        if t < win.shape[0]:
            win[t, :, :LANES] = tile
        if t > 0:
            win[t - 1, :, LANES:] = tile
    for t in range(ref_f.shape[0]):
        ref_f[t] = ordered(ref_ref, 1.0 / per_group, t)
    row = lax.broadcasted_iota(jnp.int32, shift.shape, 0)
    col = lax.broadcasted_iota(jnp.int32, shift.shape, 1)
    apart = row - jnp.where(col < LANES, col, col - (LANES - 1))
    shift[...] = apart.astype(jnp.float32).astype(jnp.bfloat16)


def correlate_pair(pair, taps_ref, weights_ref, win, ref_f, shift, wbuf, chi, clo, groups):
    tiles, chans = ref_f.shape[:2]
    step = COLS // LANES
    for k in range(2):
        wbuf[k] = weights_ref[0, 2 * pair + k].astype(jnp.float32)
    moved = []
    for k in range(2):
        offset = taps_ref[2 * pair + k]
        rest = jnp.full((1, 2 * LANES), offset & (LANES - 1), jnp.int32).astype(jnp.float32).astype(jnp.bfloat16)
        pick = jnp.where(shift[...] == rest, jnp.bfloat16(1), jnp.bfloat16(0))
        cut = win[pl.ds(offset >> 7, tiles + step)].reshape((tiles + step) * chans, 2 * LANES)
        moved.append(dot32(cut, pick))
    results = []
    for k in range(2):
        out = []
        for i in range(tiles):
            lanes = slice(i * LANES, (i + 1) * LANES)
            near = moved[k][i * chans : (i + 1) * chans]
            far = moved[k][(i + step) * chans : (i + step + 1) * chans]
            taps4 = (near[:, :LANES], near[:, LANES:], far[:, :LANES], far[:, LANES:])
            warped = None
            for tap in range(4):
                row = jnp.broadcast_to(wbuf[k, tap : tap + 1, lanes], (groups, LANES))
                row = jnp.concatenate([row] * (chans // groups), axis=0)
                warped = row * taps4[tap] if warped is None else warped + row * taps4[tap]
            product = warped * ref_f[i]
            total = product[:groups]
            for c in range(1, chans // groups):
                total = total + product[c * groups : (c + 1) * groups]
            out.append(total)
        results.append(out)
    start = pl.multiple_of((pair + 1) * 2 * groups, 2 * groups)
    for i in range(tiles):
        hi, lo = split_bf16(jnp.concatenate([results[0][i], results[1][i]], axis=0))
        chi[pl.ds(start, 2 * groups), i * LANES : (i + 1) * LANES] = hi
        clo[pl.ds(start, 2 * groups), i * LANES : (i + 1) * LANES] = lo


def filter_slab(slab, size, groups, whi, wlo, chi, clo):
    pixels = chi.shape[1]
    start = pl.multiple_of(slab * size * groups, 2 * groups)
    high = chi[pl.ds(start, (size + 4) * groups), :]
    low = clo[pl.ds(start, (size + 4) * groups), :]
    part = dot32(whi[...], high) + dot32(whi[...], low) + dot32(wlo[...], high)
    zeros = jnp.zeros((size, COLS), jnp.float32)
    width = pixels + 2 * COLS
    col = lax.broadcasted_iota(jnp.int32, (size, width), 1) & (COLS - 1)
    shifted = []
    for e in range(3):
        total = None
        for b in range(3):
            piece = part[(b * 3 + e) * size : (b * 3 + e + 1) * size]
            pads = [zeros] * (2 - b) + [piece] + [zeros] * b
            piece = jnp.concatenate(pads, axis=1)
            total = piece if total is None else total + piece
        shifted.append(total)
    left = jnp.where(col == 0, 0.0, pltpu.roll(shifted[0], 1, 1))
    right = jnp.where(col == COLS - 1, 0.0, pltpu.roll(shifted[2], width - 1, 1))
    return shifted[1] + left + right


def filter_matrix(filt_ref, whi, wlo, groups):
    cols = whi.shape[1]
    size = whi.shape[0] // 9
    group = lax.broadcasted_iota(jnp.int32, (groups, cols), 0)
    spread = ((lax.broadcasted_iota(jnp.int32, (groups, cols), 1) & (groups - 1)) == group)
    spread = spread.astype(jnp.float32).astype(jnp.bfloat16)
    plane_in = lax.broadcasted_iota(jnp.int32, (size, cols), 1) // groups
    apart = plane_in - lax.broadcasted_iota(jnp.int32, (size, cols), 0)
    for b in range(3):
        over = [[dot32(part, spread) for part in split_bf16(filt_ref[a, b])] for a in range(3)]
        for e in range(3):
            at = (b * 3 + e) * size
            for out, which in ((whi, 0), (wlo, 1)):
                total = jnp.zeros((size, cols), jnp.float32)
                for a in range(3):
                    total = jnp.where(apart == a + 1, over[a][which][e : e + 1], total)
                out[at : at + size] = total.astype(jnp.bfloat16)


def peer_at(view, tile):
    return {"view": view, "tile": tile}


def greet_peers(views, tiles, barrier):
    view, tile = lax.axis_index("view"), lax.axis_index("tile")
    for k in range(1, views):
        pl.semaphore_signal(barrier, inc=1, device_id=peer_at(lax.rem(view + k, views), tile), device_id_type=MESH)
    for k in (1, tiles - 1):
        pl.semaphore_signal(barrier, inc=1, device_id=peer_at(view, lax.rem(tile + k, tiles)), device_id_type=MESH)


def finish(views, tiles, zown, zin, hout, hin, sout, sin, slab_wait, hsend, hrecv, ssend, srecv, prob_ref, depth_ref):
    view, tile = lax.axis_index("view"), lax.axis_index("tile")
    size, width = zown.shape
    total = zown[...]
    for k in range(views - 1):
        slab_wait(k)
        total = total + zin[k]
    hout[0] = total[:, :COLS]
    hout[1] = total[:, width - COLS :]
    halo = []
    for side, k in ((0, tiles - 1), (1, 1)):
        halo.append(pltpu.make_async_remote_copy(
            src_ref=hout.at[side], dst_ref=hin.at[side], send_sem=hsend.at[side], recv_sem=hrecv.at[side],
            device_id=peer_at(view, lax.rem(tile + k, tiles)), device_id_type=MESH))
    for copy in halo:
        copy.start()
    for copy in halo:
        copy.wait()
    below = jnp.where(tile < tiles - 1, hin[0], 0.0)
    above = jnp.where(tile > 0, hin[1], 0.0)
    z = total[:, COLS : width - COLS]
    z = jnp.concatenate([z[:, :COLS] + above, z[:, COLS:-COLS], z[:, -COLS:] + below], axis=1)
    logit = 4.0 * jnp.tanh(0.5 * z)
    exps = jnp.exp(logit)
    plane = view * size + lax.broadcasted_iota(jnp.int32, exps.shape, 0)
    value = plane.astype(jnp.float32) / (size * views - 1)
    sout[0:1] = jnp.sum(exps, axis=0, keepdims=True)
    sout[1:2] = jnp.sum(exps * value, axis=0, keepdims=True)
    sums = []
    for k in range(views - 1):
        sums.append(pltpu.make_async_remote_copy(
            src_ref=sout, dst_ref=sin.at[k], send_sem=ssend.at[k], recv_sem=srecv.at[k],
            device_id=peer_at(lax.rem(view + 1 + k, views), tile), device_id_type=MESH))
    for copy in sums:
        copy.start()
    both = sout[...]
    for k, copy in enumerate(sums):
        copy.wait_recv()
        both = both + sin[k]
    prob_ref[...] = logit - jnp.log(both[0:1])
    depth_ref[...] = both[1:2] / both[0:1]
    for copy in sums:
        copy.wait_send()


def slab_copy(views, k, source, zin, zsend, zrecv):
    view, tile = lax.axis_index("view"), lax.axis_index("tile")
    return pltpu.make_async_remote_copy(
        src_ref=source, dst_ref=zin.at[k], send_sem=zsend.at[k], recv_sem=zrecv.at[k],
        device_id=peer_at(lax.rem(view + 1 + k, views), tile), device_id_type=MESH)


def prepare(taps_ref, ref_ref, src_ref, filt_ref, stage, win, ref_f, shift, chi, clo, whi, wlo, groups):
    load_features(src_ref, ref_ref, stage, win, ref_f, shift, groups)
    filter_matrix(filt_ref, whi, wlo, groups)
    edge = jnp.zeros((2 * groups, chi.shape[1]), jnp.bfloat16)
    for buf in (chi, clo):
        buf[: 2 * groups] = edge
        buf[chi.shape[0] - 2 * groups :] = edge


def whole_kernel(size, groups, views, tiles, taps_ref, ref_ref, src_ref, weights_ref, filt_ref, prob_ref, depth_ref,
                 stage, win, ref_f, shift, wbuf, chi, clo, whi, wlo, zout,
                 zin, hout, hin, sout, sin, zsend, zrecv, hsend, hrecv, ssend, srecv):
    barrier = pltpu.get_barrier_semaphore()
    greet_peers(views, tiles, barrier)
    prepare(taps_ref, ref_ref, src_ref, filt_ref, stage, win, ref_f, shift, chi, clo, whi, wlo, groups)
    pl.semaphore_wait(barrier, views + 1)
    view = lax.axis_index("view")
    pairs = weights_ref.shape[1] // 2
    half = size // 2

    def pair_step(q, _):
        pair = lax.rem(half * (view + 1) - 1 + q, pairs)
        correlate_pair(pair, taps_ref, weights_ref, win, ref_f, shift, wbuf, chi, clo, groups)
        return 0

    def slab_step(k, _):
        first = half * k + jnp.where(k > 0, 2, 0)
        last = half * (k + 1) + jnp.where(k < views - 1, 2, 1)
        lax.fori_loop(first, last, pair_step, 0)
        slab = lax.rem(view + 1 + k, views)
        zout[k] = filter_slab(slab, size, groups, whi, wlo, chi, clo)

        @pl.when(k < views - 1)
        def _():
            slab_copy(views, k, zout.at[k], zin, zsend, zrecv).start()

        return 0

    lax.fori_loop(0, views, slab_step, 0)
    copies = [slab_copy(views, k, zout.at[k], zin, zsend, zrecv) for k in range(views - 1)]
    finish(views, tiles, zout.at[views - 1], zin, hout, hin, sout, sin,
           lambda k: copies[k].wait_recv(), hsend, hrecv, ssend, srecv, prob_ref, depth_ref)
    for copy in copies:
        copy.wait_send()


def partial_scratch(chans, window, pixels, planes, groups, size):
    return [
        pltpu.VMEM((window // LANES * chans, LANES), jnp.float32),
        pltpu.VMEM((window // LANES - 1, chans, 2 * LANES), jnp.bfloat16),
        pltpu.VMEM((pixels // LANES, chans, LANES), jnp.float32),
        pltpu.VMEM((2 * LANES, 2 * LANES), jnp.bfloat16),
        pltpu.VMEM((2, 4, pixels), jnp.float32),
        pltpu.VMEM(((planes + 4) * groups, pixels), jnp.bfloat16),
        pltpu.VMEM(((planes + 4) * groups, pixels), jnp.bfloat16),
        pltpu.VMEM((9 * size, (size + 4) * groups), jnp.bfloat16),
        pltpu.VMEM((9 * size, (size + 4) * groups), jnp.bfloat16),
    ]


def exchange_scratch(views, size, pixels):
    width = pixels + 2 * COLS
    return [
        pltpu.VMEM((views - 1, size, width), jnp.float32),
        pltpu.VMEM((2, size, COLS), jnp.float32),
        pltpu.VMEM((2, size, COLS), jnp.float32),
        pltpu.VMEM((2, pixels), jnp.float32),
        pltpu.VMEM((views - 1, 2, pixels), jnp.float32),
        pltpu.SemaphoreType.DMA((views - 1,)),
        pltpu.SemaphoreType.DMA((views - 1,)),
        pltpu.SemaphoreType.DMA((2,)),
        pltpu.SemaphoreType.DMA((2,)),
        pltpu.SemaphoreType.DMA((views - 1,)),
        pltpu.SemaphoreType.DMA((views - 1,)),
    ]


def on_device(ref_feat, src_feat, taps, weights, conv_weight):
    views = lax.axis_size("view")
    tiles = lax.axis_size("tile")
    chans, pixels = ref_feat.shape
    planes = taps.shape[1]
    size = planes // views
    groups = conv_weight.shape[3]
    window = src_feat.shape[3]
    width = pixels + 2 * COLS
    vmem = pl.BlockSpec(memory_space=pltpu.VMEM)
    inputs = (taps.reshape(planes), ref_feat, src_feat, weights, conv_weight)
    in_specs = [pl.BlockSpec(memory_space=pltpu.SMEM), vmem, vmem, vmem, vmem]
    outs = (jax.ShapeDtypeStruct((size, pixels), jnp.float32), jax.ShapeDtypeStruct((1, pixels), jnp.float32))
    local = partial_scratch(chans, window, pixels, planes, groups, size)
    log_prob, depth_map = pl.pallas_call(
        functools.partial(whole_kernel, size, groups, views, tiles),
        out_shape=outs,
        in_specs=in_specs,
        out_specs=(vmem, vmem),
        scratch_shapes=local + [pltpu.VMEM((views, size, width), jnp.float32)] + exchange_scratch(views, size, pixels),
        compiler_params=pltpu.CompilerParams(collective_id=0, has_side_effects=True, vmem_limit_bytes=48 * 1024 * 1024),
    )(*inputs)
    return log_prob, depth_map[0]


def solution(mesh):
    placed = (
        P(None, "tile"),
        P("view", "tile", None, None),
        P("view", None, "tile"),
        P("view", None, None, "tile"),
        P(),
    )
    return jax.shard_map(
        on_device,
        mesh=mesh,
        in_specs=placed,
        out_specs=(P("view", "tile"), P("tile")),
        check_vma=False,
    )
```

```python
import functools

import jax
import jax.numpy as jnp
from jax import lax
from jax.experimental import pallas as pl
from jax.experimental.pallas import tpu as pltpu
from jax.sharding import PartitionSpec as P

COLS = 256
LANES = 128
MESH = pl.DeviceIdType.MESH


def split_bf16(x):
    hi = x.astype(jnp.bfloat16)
    lo = (x - hi.astype(jnp.float32)).astype(jnp.bfloat16)
    return hi, lo


def dot32(a, b):
    return lax.dot_general(a, b, (((1,), (0,)), ((), ())), preferred_element_type=jnp.float32)


def load_features(src_ref, ref_ref, stage, win, ref_f, shift, groups):
    chans = ref_ref.shape[0]
    per_group = chans // groups

    def ordered(source, scale, t):
        cut = source[:, t * LANES : (t + 1) * LANES].astype(jnp.float32)
        stage[t * chans : (t + 1) * chans] = cut * scale
        return jnp.concatenate(
            [stage[pl.ds(t * chans + c, groups, stride=per_group), :] for c in range(per_group)], axis=0
        )

    for t in range(win.shape[0] + 1):
        tile = ordered(src_ref.at[0, 0], 1.0, t).astype(jnp.bfloat16)
        if t < win.shape[0]:
            win[t, :, :LANES] = tile
        if t > 0:
            win[t - 1, :, LANES:] = tile
    for t in range(ref_f.shape[0]):
        ref_f[t] = ordered(ref_ref, 1.0 / per_group, t)
    row = lax.broadcasted_iota(jnp.int32, shift.shape, 0)
    col = lax.broadcasted_iota(jnp.int32, shift.shape, 1)
    apart = row - jnp.where(col < LANES, col, col - (LANES - 1))
    shift[...] = apart.astype(jnp.float32).astype(jnp.bfloat16)


def correlate_pair(pair, taps_ref, weights_ref, win, ref_f, shift, wbuf, chi, clo, groups):
    tiles, chans = ref_f.shape[:2]
    step = COLS // LANES
    for k in range(2):
        wbuf[k] = weights_ref[0, 2 * pair + k].astype(jnp.float32)
    moved = []
    for k in range(2):
        offset = taps_ref[2 * pair + k]
        rest = jnp.full((1, 2 * LANES), offset & (LANES - 1), jnp.int32).astype(jnp.float32).astype(jnp.bfloat16)
        pick = jnp.where(shift[...] == rest, jnp.bfloat16(1), jnp.bfloat16(0))
        cut = win[pl.ds(offset >> 7, tiles + step)].reshape((tiles + step) * chans, 2 * LANES)
        moved.append(dot32(cut, pick))
    results = []
    for k in range(2):
        out = []
        for i in range(tiles):
            lanes = slice(i * LANES, (i + 1) * LANES)
            near = moved[k][i * chans : (i + 1) * chans]
            far = moved[k][(i + step) * chans : (i + step + 1) * chans]
            taps4 = (near[:, :LANES], near[:, LANES:], far[:, :LANES], far[:, LANES:])
            warped = None
            for tap in range(4):
                row = jnp.broadcast_to(wbuf[k, tap : tap + 1, lanes], (groups, LANES))
                row = jnp.concatenate([row] * (chans // groups), axis=0)
                warped = row * taps4[tap] if warped is None else warped + row * taps4[tap]
            product = warped * ref_f[i]
            total = product[:groups]
            for c in range(1, chans // groups):
                total = total + product[c * groups : (c + 1) * groups]
            out.append(total)
        results.append(out)
    start = pl.multiple_of((pair + 1) * 2 * groups, 2 * groups)
    for i in range(tiles):
        hi, lo = split_bf16(jnp.concatenate([results[0][i], results[1][i]], axis=0))
        chi[pl.ds(start, 2 * groups), i * LANES : (i + 1) * LANES] = hi
        clo[pl.ds(start, 2 * groups), i * LANES : (i + 1) * LANES] = lo


def filter_slab(slab, size, groups, whi, wlo, chi, clo):
    pixels = chi.shape[1]
    start = pl.multiple_of(slab * size * groups, 2 * groups)
    high = chi[pl.ds(start, (size + 4) * groups), :]
    low = clo[pl.ds(start, (size + 4) * groups), :]
    part = dot32(whi[...], high) + dot32(whi[...], low) + dot32(wlo[...], high)
    zeros = jnp.zeros((size, COLS), jnp.float32)
    width = pixels + 2 * COLS
    col = lax.broadcasted_iota(jnp.int32, (size, width), 1) & (COLS - 1)
    shifted = []
    for e in range(3):
        total = None
        for b in range(3):
            piece = part[(b * 3 + e) * size : (b * 3 + e + 1) * size]
            pads = [zeros] * (2 - b) + [piece] + [zeros] * b
            piece = jnp.concatenate(pads, axis=1)
            total = piece if total is None else total + piece
        shifted.append(total)
    left = jnp.where(col == 0, 0.0, pltpu.roll(shifted[0], 1, 1))
    right = jnp.where(col == COLS - 1, 0.0, pltpu.roll(shifted[2], width - 1, 1))
    return shifted[1] + left + right


def filter_matrix(filt_ref, whi, wlo, groups):
    cols = whi.shape[1]
    size = whi.shape[0] // 9
    group = lax.broadcasted_iota(jnp.int32, (groups, cols), 0)
    spread = ((lax.broadcasted_iota(jnp.int32, (groups, cols), 1) & (groups - 1)) == group)
    spread = spread.astype(jnp.float32).astype(jnp.bfloat16)
    plane_in = lax.broadcasted_iota(jnp.int32, (size, cols), 1) // groups
    apart = plane_in - lax.broadcasted_iota(jnp.int32, (size, cols), 0)
    for b in range(3):
        over = [[dot32(part, spread) for part in split_bf16(filt_ref[a, b])] for a in range(3)]
        for e in range(3):
            at = (b * 3 + e) * size
            for out, which in ((whi, 0), (wlo, 1)):
                total = jnp.zeros((size, cols), jnp.float32)
                for a in range(3):
                    total = jnp.where(apart == a + 1, over[a][which][e : e + 1], total)
                out[at : at + size] = total.astype(jnp.bfloat16)


def peer_at(view, tile):
    return {"view": view, "tile": tile}


def greet_peers(views, tiles, barrier):
    view, tile = lax.axis_index("view"), lax.axis_index("tile")
    for k in range(1, views):
        pl.semaphore_signal(barrier, inc=1, device_id=peer_at(lax.rem(view + k, views), tile), device_id_type=MESH)
    for k in (1, tiles - 1):
        pl.semaphore_signal(barrier, inc=1, device_id=peer_at(view, lax.rem(tile + k, tiles)), device_id_type=MESH)


def finish(views, tiles, total, hout, hin, sout, sin, hsend, hrecv, ssend, srecv, prob_ref, depth_ref):
    view, tile = lax.axis_index("view"), lax.axis_index("tile")
    size, width = total.shape
    hout[0] = total[:, :COLS]
    hout[1] = total[:, width - COLS :]
    halo = []
    for side, k in ((0, tiles - 1), (1, 1)):
        halo.append(pltpu.make_async_remote_copy(
            src_ref=hout.at[side], dst_ref=hin.at[side], send_sem=hsend.at[side], recv_sem=hrecv.at[side],
            device_id=peer_at(view, lax.rem(tile + k, tiles)), device_id_type=MESH))
    for copy in halo:
        copy.start()
    for copy in halo:
        copy.wait()
    below = jnp.where(tile < tiles - 1, hin[0], 0.0)
    above = jnp.where(tile > 0, hin[1], 0.0)
    z = total[:, COLS : width - COLS]
    z = jnp.concatenate([z[:, :COLS] + above, z[:, COLS:-COLS], z[:, -COLS:] + below], axis=1)
    logit = 4.0 * jnp.tanh(0.5 * z)
    exps = jnp.exp(logit)
    plane = view * size + lax.broadcasted_iota(jnp.int32, exps.shape, 0)
    value = plane.astype(jnp.float32) / (size * views - 1)
    sout[0:1] = jnp.sum(exps, axis=0, keepdims=True)
    sout[1:2] = jnp.sum(exps * value, axis=0, keepdims=True)
    sums = []
    for k in range(views - 1):
        sums.append(pltpu.make_async_remote_copy(
            src_ref=sout, dst_ref=sin.at[k], send_sem=ssend.at[k], recv_sem=srecv.at[k],
            device_id=peer_at(lax.rem(view + 1 + k, views), tile), device_id_type=MESH))
    for copy in sums:
        copy.start()
    both = sout[...]
    for k, copy in enumerate(sums):
        copy.wait_recv()
        both = both + sin[k]
    prob_ref[...] = logit - jnp.log(both[0:1])
    depth_ref[...] = both[1:2] / both[0:1]
    for copy in sums:
        copy.wait_send()


def side_copy(i, zside, xin, xsend, xrecv):
    view, tile = lax.axis_index("view"), lax.axis_index("tile")
    return pltpu.make_async_remote_copy(
        src_ref=zside.at[i], dst_ref=xin.at[i], send_sem=xsend.at[i], recv_sem=xrecv.at[i],
        device_id=peer_at(view + 1 - 2 * lax.rem(view, 2), tile), device_id_type=MESH)


def owner_copy(views, i, zown, zin, zsend, zrecv):
    view, tile = lax.axis_index("view"), lax.axis_index("tile")
    return pltpu.make_async_remote_copy(
        src_ref=zown.at[i], dst_ref=zin.at[i], send_sem=zsend.at[i], recv_sem=zrecv.at[i],
        device_id=peer_at(lax.rem(view + 2 + 2 * i, views), tile), device_id_type=MESH)


def prepare(taps_ref, ref_ref, src_ref, filt_ref, stage, win, ref_f, shift, chi, clo, whi, wlo, groups):
    load_features(src_ref, ref_ref, stage, win, ref_f, shift, groups)
    filter_matrix(filt_ref, whi, wlo, groups)
    edge = jnp.zeros((2 * groups, chi.shape[1]), jnp.bfloat16)
    for buf in (chi, clo):
        buf[: 2 * groups] = edge
        buf[chi.shape[0] - 2 * groups :] = edge


def whole_kernel(size, groups, views, tiles, taps_ref, ref_hbm, src_hbm, weights_hbm, filt_ref, prob_ref, depth_ref,
                 ref_ref, src_ref, weights_ref, load_sem,
                 stage, win, ref_f, shift, wbuf, chi, clo, whi, wlo, zside, zown,
                 xin, zin, hout, hin, sout, sin, xsend, xrecv, zsend, zrecv, hsend, hrecv, ssend, srecv):
    loads = [
        pltpu.make_async_copy(source, target, load_sem.at[n])
        for n, (source, target) in enumerate(
            ((src_hbm, src_ref), (ref_hbm, ref_ref), (weights_hbm, weights_ref)))
    ]
    for load in loads:
        load.start()
    barrier = pltpu.get_barrier_semaphore()
    greet_peers(views, tiles, barrier)
    loads[0].wait()
    loads[1].wait()
    prepare(taps_ref, ref_ref, src_ref, filt_ref, stage, win, ref_f, shift, chi, clo, whi, wlo, groups)
    loads[2].wait()
    pl.semaphore_wait(barrier, views + 1)
    view = lax.axis_index("view")
    col = lax.rem(view, 2)
    rows = views // 2
    half = size // 2
    pairs = half * views

    def pairs_from(origin, first, last):
        def pair_step(q, _):
            pair = lax.rem(origin + q + (pairs - 1), pairs)
            correlate_pair(pair, taps_ref, weights_ref, win, ref_f, shift, wbuf, chi, clo, groups)
            return 0

        lax.fori_loop(first, last, pair_step, 0)

    def row_step(i, _):
        row = lax.rem(view // 2 + 1 + i, rows)
        origin = row * size
        final = jnp.where(i < rows - 1, 1, 0)
        low, high = jnp.where(col == 0, half, 2), jnp.where(col == 0, size + final + 1, half + 2)

        @pl.when(i == 0)
        def _():
            pairs_from(origin, 0, 2)

        pairs_from(origin, low, high)
        zside[i] = filter_slab(2 * row + 1 - col, size, groups, whi, wlo, chi, clo)
        side_copy(i, zside, xin, xsend, xrecv).start()
        low, high = jnp.where(col == 0, 2, half + 2), jnp.where(col == 0, half, size + final + 1)
        pairs_from(origin, low, high)
        own = filter_slab(2 * row + col, size, groups, whi, wlo, chi, clo)
        side_copy(i, zside, xin, xsend, xrecv).wait_recv()
        zown[i] = own + xin[i]

        @pl.when(i < rows - 1)
        def _():
            owner_copy(views, i, zown, zin, zsend, zrecv).start()

        return 0

    lax.fori_loop(0, rows, row_step, 0)
    total = zown[rows - 1]
    copies = [owner_copy(views, i, zown, zin, zsend, zrecv) for i in range(rows - 1)]
    for i, copy in enumerate(copies):
        copy.wait_recv()
        total = total + zin[i]
    finish(views, tiles, total, hout, hin, sout, sin, hsend, hrecv, ssend, srecv, prob_ref, depth_ref)
    for copy in copies:
        copy.wait_send()
    for i in range(rows):
        side_copy(i, zside, xin, xsend, xrecv).wait_send()


def partial_scratch(chans, window, pixels, planes, groups, size):
    return [
        pltpu.VMEM((window // LANES * chans, LANES), jnp.float32),
        pltpu.VMEM((window // LANES - 1, chans, 2 * LANES), jnp.bfloat16),
        pltpu.VMEM((pixels // LANES, chans, LANES), jnp.float32),
        pltpu.VMEM((2 * LANES, 2 * LANES), jnp.bfloat16),
        pltpu.VMEM((2, 4, pixels), jnp.float32),
        pltpu.VMEM(((planes + 4) * groups, pixels), jnp.bfloat16),
        pltpu.VMEM(((planes + 4) * groups, pixels), jnp.bfloat16),
        pltpu.VMEM((9 * size, (size + 4) * groups), jnp.bfloat16),
        pltpu.VMEM((9 * size, (size + 4) * groups), jnp.bfloat16),
    ]


def exchange_scratch(views, size, pixels):
    width = pixels + 2 * COLS
    rows = views // 2
    return [
        pltpu.VMEM((rows, size, width), jnp.float32),
        pltpu.VMEM((rows, size, width), jnp.float32),
        pltpu.VMEM((rows, size, width), jnp.float32),
        pltpu.VMEM((rows - 1, size, width), jnp.float32),
        pltpu.VMEM((2, size, COLS), jnp.float32),
        pltpu.VMEM((2, size, COLS), jnp.float32),
        pltpu.VMEM((2, pixels), jnp.float32),
        pltpu.VMEM((views - 1, 2, pixels), jnp.float32),
        pltpu.SemaphoreType.DMA((rows,)),
        pltpu.SemaphoreType.DMA((rows,)),
        pltpu.SemaphoreType.DMA((rows - 1,)),
        pltpu.SemaphoreType.DMA((rows - 1,)),
        pltpu.SemaphoreType.DMA((2,)),
        pltpu.SemaphoreType.DMA((2,)),
        pltpu.SemaphoreType.DMA((views - 1,)),
        pltpu.SemaphoreType.DMA((views - 1,)),
    ]


def on_device(ref_feat, src_feat, taps, weights, conv_weight):
    views = lax.axis_size("view")
    tiles = lax.axis_size("tile")
    chans, pixels = ref_feat.shape
    planes = taps.shape[1]
    size = planes // views
    groups = conv_weight.shape[3]
    window = src_feat.shape[3]
    vmem = pl.BlockSpec(memory_space=pltpu.VMEM)
    anywhere = pl.BlockSpec(memory_space=pl.ANY)
    inputs = (taps.reshape(planes), ref_feat, src_feat, weights, conv_weight)
    in_specs = [pl.BlockSpec(memory_space=pltpu.SMEM), anywhere, anywhere, anywhere, vmem]
    outs = (jax.ShapeDtypeStruct((size, pixels), jnp.float32), jax.ShapeDtypeStruct((1, pixels), jnp.float32))
    fetched = [pltpu.VMEM(x.shape, x.dtype) for x in (ref_feat, src_feat, weights)] + [pltpu.SemaphoreType.DMA((3,))]
    local = partial_scratch(chans, window, pixels, planes, groups, size)
    log_prob, depth_map = pl.pallas_call(
        functools.partial(whole_kernel, size, groups, views, tiles),
        out_shape=outs,
        in_specs=in_specs,
        out_specs=(vmem, vmem),
        scratch_shapes=fetched + local + exchange_scratch(views, size, pixels),
        compiler_params=pltpu.CompilerParams(collective_id=0, has_side_effects=True, vmem_limit_bytes=56 * 1024 * 1024),
    )(*inputs)
    return log_prob, depth_map[0]


def solution(mesh):
    placed = (
        P(None, "tile"),
        P("view", "tile", None, None),
        P("view", None, "tile"),
        P("view", None, None, "tile"),
        P(),
    )
    return jax.shard_map(
        on_device,
        mesh=mesh,
        in_specs=placed,
        out_specs=(P("view", "tile"), P("tile")),
        check_vma=False,
    )
```

```python
import functools

import jax
import jax.numpy as jnp
from jax import lax
from jax.experimental import pallas as pl
from jax.experimental.pallas import tpu as pltpu
from jax.sharding import PartitionSpec as P

COLS = 256
LANES = 128
MESH = pl.DeviceIdType.MESH


def split_bf16(x):
    hi = x.astype(jnp.bfloat16)
    lo = (x - hi.astype(jnp.float32)).astype(jnp.bfloat16)
    return hi, lo


def dot32(a, b):
    return lax.dot_general(a, b, (((1,), (0,)), ((), ())), preferred_element_type=jnp.float32)


def load_features(src_ref, ref_ref, stage, win, ref_f, shift, groups):
    chans = ref_ref.shape[0]
    per_group = chans // groups

    def ordered(source, scale, t):
        cut = source[:, t * LANES : (t + 1) * LANES].astype(jnp.float32)
        stage[t * chans : (t + 1) * chans] = cut * scale
        return jnp.concatenate(
            [stage[pl.ds(t * chans + c, groups, stride=per_group), :] for c in range(per_group)], axis=0
        )

    for t in range(win.shape[0] + 1):
        tile = ordered(src_ref.at[0, 0], 1.0, t).astype(jnp.bfloat16)
        if t < win.shape[0]:
            win[t, :, :LANES] = tile
        if t > 0:
            win[t - 1, :, LANES:] = tile
    for t in range(ref_f.shape[0]):
        ref_f[t] = ordered(ref_ref, 1.0 / per_group, t)
    row = lax.broadcasted_iota(jnp.int32, shift.shape, 0)
    col = lax.broadcasted_iota(jnp.int32, shift.shape, 1)
    apart = row - jnp.where(col < LANES, col, col - (LANES - 1))
    shift[...] = apart.astype(jnp.float32).astype(jnp.bfloat16)


def correlate_pair(pair, taps_ref, weights_ref, win, ref_f, shift, wbuf, chi, clo, groups):
    tiles, chans = ref_f.shape[:2]
    step = COLS // LANES
    for k in range(2):
        wbuf[k] = weights_ref[0, 2 * pair + k].astype(jnp.float32)
    moved = []
    for k in range(2):
        offset = taps_ref[2 * pair + k]
        rest = jnp.full((1, 2 * LANES), offset & (LANES - 1), jnp.int32).astype(jnp.float32).astype(jnp.bfloat16)
        pick = jnp.where(shift[...] == rest, jnp.bfloat16(1), jnp.bfloat16(0))
        cut = win[pl.ds(offset >> 7, tiles + step)].reshape((tiles + step) * chans, 2 * LANES)
        moved.append(dot32(cut, pick))

    def tap_row(k, tap, t):
        row = jnp.broadcast_to(wbuf[k, tap : tap + 1, t * LANES : (t + 1) * LANES], (groups, LANES))
        return jnp.concatenate([row] * (chans // groups), axis=0)

    results = []
    for k in range(2):
        out, near = [], []
        for t in range(tiles + step):
            here = moved[k][t * chans : (t + 1) * chans]
            sides = (here[:, :LANES], here[:, LANES:])
            if t >= step:
                warped = near[t - step] + tap_row(k, 2, t - step) * sides[0] + tap_row(k, 3, t - step) * sides[1]
                product = warped * ref_f[t - step]
                total = product[:groups]
                for c in range(1, chans // groups):
                    total = total + product[c * groups : (c + 1) * groups]
                out.append(total)
            if t < tiles:
                near.append(tap_row(k, 0, t) * sides[0] + tap_row(k, 1, t) * sides[1])
        results.append(out)
    start = pl.multiple_of((pair + 1) * 2 * groups, 2 * groups)
    for i in range(tiles):
        hi, lo = split_bf16(jnp.concatenate([results[0][i], results[1][i]], axis=0))
        chi[pl.ds(start, 2 * groups), i * LANES : (i + 1) * LANES] = hi
        clo[pl.ds(start, 2 * groups), i * LANES : (i + 1) * LANES] = lo


def filter_slab(slab, size, groups, wboth, chi, clo):
    pixels = chi.shape[1]
    start = pl.multiple_of(slab * size * groups, 2 * groups)
    high = chi[pl.ds(start, (size + 4) * groups), :]
    low = clo[pl.ds(start, (size + 4) * groups), :]
    both = dot32(wboth[...], high)
    taps9 = 9 * size
    part = both[:taps9] + both[taps9:] + dot32(wboth[:taps9], low)
    zeros = jnp.zeros((size, COLS), jnp.float32)
    width = pixels + 2 * COLS
    col = lax.broadcasted_iota(jnp.int32, (size, width), 1) & (COLS - 1)
    shifted = []
    for e in range(3):
        total = None
        for b in range(3):
            piece = part[(b * 3 + e) * size : (b * 3 + e + 1) * size]
            pads = [zeros] * (2 - b) + [piece] + [zeros] * b
            piece = jnp.concatenate(pads, axis=1)
            total = piece if total is None else total + piece
        shifted.append(total)
    left = jnp.where(col == 0, 0.0, pltpu.roll(shifted[0], 1, 1))
    right = jnp.where(col == COLS - 1, 0.0, pltpu.roll(shifted[2], width - 1, 1))
    return shifted[1] + left + right


def filter_matrix(filt_ref, wboth, groups):
    cols = wboth.shape[1]
    size = wboth.shape[0] // 18
    group = lax.broadcasted_iota(jnp.int32, (groups, cols), 0)
    spread = ((lax.broadcasted_iota(jnp.int32, (groups, cols), 1) & (groups - 1)) == group)
    spread = spread.astype(jnp.float32).astype(jnp.bfloat16)
    plane_in = lax.broadcasted_iota(jnp.int32, (size, cols), 1) // groups
    apart = plane_in - lax.broadcasted_iota(jnp.int32, (size, cols), 0)
    for b in range(3):
        over = [[dot32(part, spread) for part in split_bf16(filt_ref[a, b])] for a in range(3)]
        for e in range(3):
            for which in range(2):
                total = jnp.zeros((size, cols), jnp.float32)
                for a in range(3):
                    total = jnp.where(apart == a + 1, over[a][which][e : e + 1], total)
                at = ((which * 3 + b) * 3 + e) * size
                wboth[at : at + size] = total.astype(jnp.bfloat16)


def peer_at(view, tile):
    return {"view": view, "tile": tile}


def greet_peers(views, tiles, barrier):
    view, tile = lax.axis_index("view"), lax.axis_index("tile")
    for k in range(1, views):
        pl.semaphore_signal(barrier, inc=1, device_id=peer_at(lax.rem(view + k, views), tile), device_id_type=MESH)
    for k in (1, tiles - 1):
        pl.semaphore_signal(barrier, inc=1, device_id=peer_at(view, lax.rem(tile + k, tiles)), device_id_type=MESH)


def finish(views, tiles, total, hout, hin, sout, sin, hsend, hrecv, ssend, srecv, prob_ref, depth_ref):
    view, tile = lax.axis_index("view"), lax.axis_index("tile")
    size, width = total.shape
    hout[0] = total[:, :COLS]
    hout[1] = total[:, width - COLS :]
    halo = []
    for side, k in ((0, tiles - 1), (1, 1)):
        halo.append(pltpu.make_async_remote_copy(
            src_ref=hout.at[side], dst_ref=hin.at[side], send_sem=hsend.at[side], recv_sem=hrecv.at[side],
            device_id=peer_at(view, lax.rem(tile + k, tiles)), device_id_type=MESH))
    for copy in halo:
        copy.start()
    for copy in halo:
        copy.wait()
    below = jnp.where(tile < tiles - 1, hin[0], 0.0)
    above = jnp.where(tile > 0, hin[1], 0.0)
    z = total[:, COLS : width - COLS]
    z = jnp.concatenate([z[:, :COLS] + above, z[:, COLS:-COLS], z[:, -COLS:] + below], axis=1)
    logit = 4.0 * jnp.tanh(0.5 * z)
    exps = jnp.exp(logit)
    plane = view * size + lax.broadcasted_iota(jnp.int32, exps.shape, 0)
    value = plane.astype(jnp.float32) / (size * views - 1)
    sout[0:1] = jnp.sum(exps, axis=0, keepdims=True)
    sout[1:2] = jnp.sum(exps * value, axis=0, keepdims=True)
    sums = []
    for k in range(views - 1):
        sums.append(pltpu.make_async_remote_copy(
            src_ref=sout, dst_ref=sin.at[k], send_sem=ssend.at[k], recv_sem=srecv.at[k],
            device_id=peer_at(lax.rem(view + 1 + k, views), tile), device_id_type=MESH))
    for copy in sums:
        copy.start()
    both = sout[...]
    for k, copy in enumerate(sums):
        copy.wait_recv()
        both = both + sin[k]
    prob_ref[...] = logit - jnp.log(both[0:1])
    depth_ref[...] = both[1:2] / both[0:1]
    for copy in sums:
        copy.wait_send()


def side_copy(i, zside, xin, xsend, xrecv):
    view, tile = lax.axis_index("view"), lax.axis_index("tile")
    return pltpu.make_async_remote_copy(
        src_ref=zside.at[i], dst_ref=xin.at[i], send_sem=xsend.at[i], recv_sem=xrecv.at[i],
        device_id=peer_at(view + 1 - 2 * lax.rem(view, 2), tile), device_id_type=MESH)


def owner_copy(views, i, zown, zin, zsend, zrecv):
    view, tile = lax.axis_index("view"), lax.axis_index("tile")
    return pltpu.make_async_remote_copy(
        src_ref=zown.at[i], dst_ref=zin.at[i], send_sem=zsend.at[i], recv_sem=zrecv.at[i],
        device_id=peer_at(lax.rem(view + 2 + 2 * i, views), tile), device_id_type=MESH)


def prepare(taps_ref, ref_ref, src_ref, filt_ref, stage, win, ref_f, shift, chi, clo, wboth, groups):
    load_features(src_ref, ref_ref, stage, win, ref_f, shift, groups)
    filter_matrix(filt_ref, wboth, groups)
    edge = jnp.zeros((2 * groups, chi.shape[1]), jnp.bfloat16)
    for buf in (chi, clo):
        buf[: 2 * groups] = edge
        buf[chi.shape[0] - 2 * groups :] = edge


def whole_kernel(size, groups, views, tiles, taps_ref, ref_hbm, src_hbm, weights_hbm, filt_ref, prob_ref, depth_ref,
                 ref_ref, src_ref, weights_ref, load_sem,
                 stage, win, ref_f, shift, wbuf, chi, clo, wboth, zside, zown,
                 xin, zin, hout, hin, sout, sin, xsend, xrecv, zsend, zrecv, hsend, hrecv, ssend, srecv):
    loads = [
        pltpu.make_async_copy(source, target, load_sem.at[n])
        for n, (source, target) in enumerate(
            ((src_hbm, src_ref), (ref_hbm, ref_ref), (weights_hbm, weights_ref)))
    ]
    for load in loads:
        load.start()
    barrier = pltpu.get_barrier_semaphore()
    greet_peers(views, tiles, barrier)
    loads[0].wait()
    loads[1].wait()
    prepare(taps_ref, ref_ref, src_ref, filt_ref, stage, win, ref_f, shift, chi, clo, wboth, groups)
    loads[2].wait()
    pl.semaphore_wait(barrier, views + 1)
    view = lax.axis_index("view")
    col = lax.rem(view, 2)
    rows = views // 2
    half = size // 2
    pairs = half * views

    def pairs_from(origin, first, last):
        def pair_step(q, _):
            pair = lax.rem(origin + q + (pairs - 1), pairs)
            correlate_pair(pair, taps_ref, weights_ref, win, ref_f, shift, wbuf, chi, clo, groups)
            return 0

        lax.fori_loop(first, last, pair_step, 0)

    def row_step(i, _):
        row = lax.rem(view // 2 + 1 + i, rows)
        origin = row * size
        final = jnp.where(i < rows - 1, 1, 0)
        low, high = jnp.where(col == 0, half, 2), jnp.where(col == 0, size + final + 1, half + 2)

        @pl.when(i == 0)
        def _():
            pairs_from(origin, 0, 2)

        pairs_from(origin, low, high)
        zside[i] = filter_slab(2 * row + 1 - col, size, groups, wboth, chi, clo)
        side_copy(i, zside, xin, xsend, xrecv).start()
        low, high = jnp.where(col == 0, 2, half + 2), jnp.where(col == 0, half, size + final + 1)
        pairs_from(origin, low, high)
        own = filter_slab(2 * row + col, size, groups, wboth, chi, clo)
        side_copy(i, zside, xin, xsend, xrecv).wait_recv()
        zown[i] = own + xin[i]

        @pl.when(i < rows - 1)
        def _():
            owner_copy(views, i, zown, zin, zsend, zrecv).start()

        return 0

    lax.fori_loop(0, rows, row_step, 0)
    total = zown[rows - 1]
    copies = [owner_copy(views, i, zown, zin, zsend, zrecv) for i in range(rows - 1)]
    for i, copy in enumerate(copies):
        copy.wait_recv()
        total = total + zin[i]
    finish(views, tiles, total, hout, hin, sout, sin, hsend, hrecv, ssend, srecv, prob_ref, depth_ref)
    for copy in copies:
        copy.wait_send()
    for i in range(rows):
        side_copy(i, zside, xin, xsend, xrecv).wait_send()


def partial_scratch(chans, window, pixels, planes, groups, size):
    return [
        pltpu.VMEM((window // LANES * chans, LANES), jnp.float32),
        pltpu.VMEM((window // LANES - 1, chans, 2 * LANES), jnp.bfloat16),
        pltpu.VMEM((pixels // LANES, chans, LANES), jnp.float32),
        pltpu.VMEM((2 * LANES, 2 * LANES), jnp.bfloat16),
        pltpu.VMEM((2, 4, pixels), jnp.float32),
        pltpu.VMEM(((planes + 4) * groups, pixels), jnp.bfloat16),
        pltpu.VMEM(((planes + 4) * groups, pixels), jnp.bfloat16),
        pltpu.VMEM((18 * size, (size + 4) * groups), jnp.bfloat16),
    ]


def exchange_scratch(views, size, pixels):
    width = pixels + 2 * COLS
    rows = views // 2
    return [
        pltpu.VMEM((rows, size, width), jnp.float32),
        pltpu.VMEM((rows, size, width), jnp.float32),
        pltpu.VMEM((rows, size, width), jnp.float32),
        pltpu.VMEM((rows - 1, size, width), jnp.float32),
        pltpu.VMEM((2, size, COLS), jnp.float32),
        pltpu.VMEM((2, size, COLS), jnp.float32),
        pltpu.VMEM((2, pixels), jnp.float32),
        pltpu.VMEM((views - 1, 2, pixels), jnp.float32),
        pltpu.SemaphoreType.DMA((rows,)),
        pltpu.SemaphoreType.DMA((rows,)),
        pltpu.SemaphoreType.DMA((rows - 1,)),
        pltpu.SemaphoreType.DMA((rows - 1,)),
        pltpu.SemaphoreType.DMA((2,)),
        pltpu.SemaphoreType.DMA((2,)),
        pltpu.SemaphoreType.DMA((views - 1,)),
        pltpu.SemaphoreType.DMA((views - 1,)),
    ]


def on_device(ref_feat, src_feat, taps, weights, conv_weight):
    views = lax.axis_size("view")
    tiles = lax.axis_size("tile")
    chans, pixels = ref_feat.shape
    planes = taps.shape[1]
    size = planes // views
    groups = conv_weight.shape[3]
    window = src_feat.shape[3]
    vmem = pl.BlockSpec(memory_space=pltpu.VMEM)
    anywhere = pl.BlockSpec(memory_space=pl.ANY)
    inputs = (taps.reshape(planes), ref_feat, src_feat, weights, conv_weight)
    in_specs = [pl.BlockSpec(memory_space=pltpu.SMEM), anywhere, anywhere, anywhere, vmem]
    outs = (jax.ShapeDtypeStruct((size, pixels), jnp.float32), jax.ShapeDtypeStruct((1, pixels), jnp.float32))
    fetched = [pltpu.VMEM(x.shape, x.dtype) for x in (ref_feat, src_feat, weights)] + [pltpu.SemaphoreType.DMA((3,))]
    local = partial_scratch(chans, window, pixels, planes, groups, size)
    log_prob, depth_map = pl.pallas_call(
        functools.partial(whole_kernel, size, groups, views, tiles),
        out_shape=outs,
        in_specs=in_specs,
        out_specs=(vmem, vmem),
        scratch_shapes=fetched + local + exchange_scratch(views, size, pixels),
        compiler_params=pltpu.CompilerParams(collective_id=0, has_side_effects=True, vmem_limit_bytes=56 * 1024 * 1024),
    )(*inputs)
    return log_prob, depth_map[0]


def solution(mesh):
    placed = (
        P(None, "tile"),
        P("view", "tile", None, None),
        P("view", None, "tile"),
        P("view", None, None, "tile"),
        P(),
    )
    return jax.shard_map(
        on_device,
        mesh=mesh,
        in_specs=placed,
        out_specs=(P("view", "tile"), P("tile")),
        check_vma=False,
    )
```

```python
import functools

import jax
import jax.numpy as jnp
from jax import lax
from jax.experimental import pallas as pl
from jax.experimental.pallas import tpu as pltpu
from jax.sharding import PartitionSpec as P

COLS = 256
LANES = 128
MESH = pl.DeviceIdType.MESH


def split_bf16(x):
    hi = x.astype(jnp.bfloat16)
    lo = (x - hi.astype(jnp.float32)).astype(jnp.bfloat16)
    return hi, lo


def dot32(a, b):
    return lax.dot_general(a, b, (((1,), (0,)), ((), ())), preferred_element_type=jnp.float32)


def load_features(src_ref, ref_ref, stage, win, ref_f, shift, groups):
    chans = ref_ref.shape[0]
    per_group = chans // groups

    def ordered(source, scale, t):
        cut = source[:, t * LANES : (t + 1) * LANES].astype(jnp.float32)
        stage[t * chans : (t + 1) * chans] = cut * scale
        return jnp.concatenate(
            [stage[pl.ds(t * chans + c, groups, stride=per_group), :] for c in range(per_group)], axis=0
        )

    for t in range(win.shape[0] + 1):
        tile = ordered(src_ref.at[0, 0], 1.0, t).astype(jnp.bfloat16)
        if t < win.shape[0]:
            win[t, :, :LANES] = tile
        if t > 0:
            win[t - 1, :, LANES:] = tile
    for t in range(ref_f.shape[0]):
        ref_f[t] = ordered(ref_ref, 1.0 / per_group, t)
    row = lax.broadcasted_iota(jnp.int32, shift.shape, 0)
    col = lax.broadcasted_iota(jnp.int32, shift.shape, 1)
    apart = row - jnp.where(col < LANES, col, col - (LANES - 1))
    shift[...] = apart.astype(jnp.float32).astype(jnp.bfloat16)


def correlate_pair(pair, taps_ref, weights_ref, win, ref_f, shift, wbuf, chi, clo, groups):
    tiles, chans = ref_f.shape[:2]
    step = COLS // LANES
    for k in range(2):
        wbuf[k] = weights_ref[0, 2 * pair + k].astype(jnp.float32)
    moved = []
    for k in range(2):
        offset = taps_ref[2 * pair + k]
        rest = jnp.full((1, 2 * LANES), offset & (LANES - 1), jnp.int32).astype(jnp.float32).astype(jnp.bfloat16)
        pick = jnp.where(shift[...] == rest, jnp.bfloat16(1), jnp.bfloat16(0))
        cut = win[pl.ds(offset >> 7, tiles + step)].reshape((tiles + step) * chans, 2 * LANES)
        moved.append(dot32(cut, pick))

    def tap_row(k, tap, t):
        row = jnp.broadcast_to(wbuf[k, tap : tap + 1, t * LANES : (t + 1) * LANES], (groups, LANES))
        return jnp.concatenate([row] * (chans // groups), axis=0)

    results = []
    for k in range(2):
        out, near = [], []
        for t in range(tiles + step):
            here = moved[k][t * chans : (t + 1) * chans]
            sides = (here[:, :LANES], here[:, LANES:])
            if t >= step:
                warped = near[t - step] + tap_row(k, 2, t - step) * sides[0] + tap_row(k, 3, t - step) * sides[1]
                product = warped * ref_f[t - step]
                total = product[:groups]
                for c in range(1, chans // groups):
                    total = total + product[c * groups : (c + 1) * groups]
                out.append(total)
            if t < tiles:
                near.append(tap_row(k, 0, t) * sides[0] + tap_row(k, 1, t) * sides[1])
        results.append(out)
    start = pl.multiple_of((pair + 1) * 2 * groups, 2 * groups)
    for i in range(tiles):
        hi, lo = split_bf16(jnp.concatenate([results[0][i], results[1][i]], axis=0))
        chi[pl.ds(start, 2 * groups), i * LANES : (i + 1) * LANES] = hi
        clo[pl.ds(start, 2 * groups), i * LANES : (i + 1) * LANES] = lo


def filter_slab(slab, size, groups, wboth, chi, clo):
    pixels = chi.shape[1]
    start = pl.multiple_of(slab * size * groups, 2 * groups)
    high = chi[pl.ds(start, (size + 4) * groups), :]
    low = clo[pl.ds(start, (size + 4) * groups), :]
    both = dot32(wboth[...], high)
    taps9 = 9 * size
    part = both[:taps9] + both[taps9:] + dot32(wboth[:taps9], low)
    zeros = jnp.zeros((size, COLS), jnp.float32)
    width = pixels + 2 * COLS
    col = lax.broadcasted_iota(jnp.int32, (size, width), 1) & (COLS - 1)
    shifted = []
    for e in range(3):
        total = None
        for b in range(3):
            piece = part[(b * 3 + e) * size : (b * 3 + e + 1) * size]
            pads = [zeros] * (2 - b) + [piece] + [zeros] * b
            piece = jnp.concatenate(pads, axis=1)
            total = piece if total is None else total + piece
        shifted.append(total)
    left = jnp.where(col == 0, 0.0, pltpu.roll(shifted[0], 1, 1))
    right = jnp.where(col == COLS - 1, 0.0, pltpu.roll(shifted[2], width - 1, 1))
    return shifted[1] + left + right


def filter_matrix(filt_ref, wboth, groups):
    cols = wboth.shape[1]
    size = wboth.shape[0] // 18
    group = lax.broadcasted_iota(jnp.int32, (groups, cols), 0)
    spread = ((lax.broadcasted_iota(jnp.int32, (groups, cols), 1) & (groups - 1)) == group)
    spread = spread.astype(jnp.float32).astype(jnp.bfloat16)
    plane_in = lax.broadcasted_iota(jnp.int32, (size, cols), 1) // groups
    apart = plane_in - lax.broadcasted_iota(jnp.int32, (size, cols), 0)
    for b in range(3):
        over = [[dot32(part, spread) for part in split_bf16(filt_ref[a, b])] for a in range(3)]
        for e in range(3):
            for which in range(2):
                total = jnp.zeros((size, cols), jnp.float32)
                for a in range(3):
                    total = jnp.where(apart == a + 1, over[a][which][e : e + 1], total)
                at = ((which * 3 + b) * 3 + e) * size
                wboth[at : at + size] = total.astype(jnp.bfloat16)


def peer_at(view, tile):
    return {"view": view, "tile": tile}


def greet_peers(views, tiles, barrier):
    view, tile = lax.axis_index("view"), lax.axis_index("tile")
    for k in range(1, views):
        pl.semaphore_signal(barrier, inc=1, device_id=peer_at(lax.rem(view + k, views), tile), device_id_type=MESH)
    for k in (1, tiles - 1):
        pl.semaphore_signal(barrier, inc=1, device_id=peer_at(view, lax.rem(tile + k, tiles)), device_id_type=MESH)


def finish(views, tiles, total, hout, hin, sout, sin, hsend, hrecv, ssend, srecv, prob_ref, depth_ref):
    view, tile = lax.axis_index("view"), lax.axis_index("tile")
    size, width = total.shape
    hout[0] = total[:, :COLS]
    hout[1] = total[:, width - COLS :]
    halo = []
    for side, k in ((0, tiles - 1), (1, 1)):
        halo.append(pltpu.make_async_remote_copy(
            src_ref=hout.at[side], dst_ref=hin.at[side], send_sem=hsend.at[side], recv_sem=hrecv.at[side],
            device_id=peer_at(view, lax.rem(tile + k, tiles)), device_id_type=MESH))
    for copy in halo:
        copy.start()
    for copy in halo:
        copy.wait()
    below = jnp.where(tile < tiles - 1, hin[0], 0.0)
    above = jnp.where(tile > 0, hin[1], 0.0)
    z = total[:, COLS : width - COLS]
    z = jnp.concatenate([z[:, :COLS] + above, z[:, COLS:-COLS], z[:, -COLS:] + below], axis=1)
    logit = 4.0 * jnp.tanh(0.5 * z)
    exps = jnp.exp(logit)
    plane = view * size + lax.broadcasted_iota(jnp.int32, exps.shape, 0)
    value = plane.astype(jnp.float32) / (size * views - 1)
    sout[0:1] = jnp.sum(exps, axis=0, keepdims=True)
    sout[1:2] = jnp.sum(exps * value, axis=0, keepdims=True)
    sums = []
    for k in range(views - 1):
        sums.append(pltpu.make_async_remote_copy(
            src_ref=sout, dst_ref=sin.at[k], send_sem=ssend.at[k], recv_sem=srecv.at[k],
            device_id=peer_at(lax.rem(view + 1 + k, views), tile), device_id_type=MESH))
    for copy in sums:
        copy.start()
    both = sout[...]
    for k, copy in enumerate(sums):
        copy.wait_recv()
        both = both + sin[k]
    prob_ref[...] = logit - jnp.log(both[0:1])
    depth_ref[...] = both[1:2] / both[0:1]
    for copy in sums:
        copy.wait_send()


def side_copy(i, zside, xin, xsend, xrecv):
    view, tile = lax.axis_index("view"), lax.axis_index("tile")
    return pltpu.make_async_remote_copy(
        src_ref=zside.at[i], dst_ref=xin.at[i], send_sem=xsend.at[i], recv_sem=xrecv.at[i],
        device_id=peer_at(view + 1 - 2 * lax.rem(view, 2), tile), device_id_type=MESH)


def owner_copy(views, i, zown, zin, zsend, zrecv):
    view, tile = lax.axis_index("view"), lax.axis_index("tile")
    return pltpu.make_async_remote_copy(
        src_ref=zown.at[i], dst_ref=zin.at[i], send_sem=zsend.at[i], recv_sem=zrecv.at[i],
        device_id=peer_at(lax.rem(view + 2 + 2 * i, views), tile), device_id_type=MESH)


def prepare(taps_ref, ref_ref, src_ref, filt_ref, stage, win, ref_f, shift, chi, clo, wboth, groups):
    load_features(src_ref, ref_ref, stage, win, ref_f, shift, groups)
    filter_matrix(filt_ref, wboth, groups)
    edge = jnp.zeros((2 * groups, chi.shape[1]), jnp.bfloat16)
    for buf in (chi, clo):
        buf[: 2 * groups] = edge
        buf[chi.shape[0] - 2 * groups :] = edge


def whole_kernel(size, groups, views, tiles, taps_ref, ref_hbm, src_hbm, weights_hbm, filt_ref, prob_ref, depth_ref,
                 ref_ref, src_ref, weights_ref, load_sem,
                 stage, win, ref_f, shift, wbuf, chi, clo, wboth, zside, zown,
                 xin, zin, hout, hin, sout, sin, xsend, xrecv, zsend, zrecv, hsend, hrecv, ssend, srecv):
    loads = [
        pltpu.make_async_copy(source, target, load_sem.at[n])
        for n, (source, target) in enumerate(
            ((src_hbm, src_ref), (ref_hbm, ref_ref), (weights_hbm, weights_ref)))
    ]
    for load in loads:
        load.start()
    barrier = pltpu.get_barrier_semaphore()
    greet_peers(views, tiles, barrier)
    loads[0].wait()
    loads[1].wait()
    prepare(taps_ref, ref_ref, src_ref, filt_ref, stage, win, ref_f, shift, chi, clo, wboth, groups)
    loads[2].wait()
    view = lax.axis_index("view")
    col = lax.rem(view, 2)
    rows = views // 2
    half = size // 2
    pairs = half * views

    def pairs_from(origin, first, last):
        def pair_step(q, _):
            pair = lax.rem(origin + q + (pairs - 1), pairs)
            correlate_pair(pair, taps_ref, weights_ref, win, ref_f, shift, wbuf, chi, clo, groups)
            return 0

        lax.fori_loop(first, last, pair_step, 0)

    def row_step(i, _):
        row = lax.rem(view // 2 + 1 + i, rows)
        origin = row * size
        final = jnp.where(i < rows - 1, 1, 0)
        low, high = jnp.where(col == 0, half, 2), jnp.where(col == 0, size + final + 1, half + 2)

        @pl.when(i == 0)
        def _():
            pairs_from(origin, 0, 2)

        pairs_from(origin, low, high)
        zside[i] = filter_slab(2 * row + 1 - col, size, groups, wboth, chi, clo)

        @pl.when(i == 0)
        def _():
            pl.semaphore_wait(barrier, views + 1)

        side_copy(i, zside, xin, xsend, xrecv).start()
        low, high = jnp.where(col == 0, 2, half + 2), jnp.where(col == 0, half, size + final + 1)
        pairs_from(origin, low, high)
        own = filter_slab(2 * row + col, size, groups, wboth, chi, clo)
        side_copy(i, zside, xin, xsend, xrecv).wait_recv()
        zown[i] = own + xin[i]

        @pl.when(i < rows - 1)
        def _():
            owner_copy(views, i, zown, zin, zsend, zrecv).start()

        return 0

    lax.fori_loop(0, rows, row_step, 0)
    total = zown[rows - 1]
    copies = [owner_copy(views, i, zown, zin, zsend, zrecv) for i in range(rows - 1)]
    for i, copy in enumerate(copies):
        copy.wait_recv()
        total = total + zin[i]
    finish(views, tiles, total, hout, hin, sout, sin, hsend, hrecv, ssend, srecv, prob_ref, depth_ref)
    for copy in copies:
        copy.wait_send()
    for i in range(rows):
        side_copy(i, zside, xin, xsend, xrecv).wait_send()


def partial_scratch(chans, window, pixels, planes, groups, size):
    return [
        pltpu.VMEM((window // LANES * chans, LANES), jnp.float32),
        pltpu.VMEM((window // LANES - 1, chans, 2 * LANES), jnp.bfloat16),
        pltpu.VMEM((pixels // LANES, chans, LANES), jnp.float32),
        pltpu.VMEM((2 * LANES, 2 * LANES), jnp.bfloat16),
        pltpu.VMEM((2, 4, pixels), jnp.float32),
        pltpu.VMEM(((planes + 4) * groups, pixels), jnp.bfloat16),
        pltpu.VMEM(((planes + 4) * groups, pixels), jnp.bfloat16),
        pltpu.VMEM((18 * size, (size + 4) * groups), jnp.bfloat16),
    ]


def exchange_scratch(views, size, pixels):
    width = pixels + 2 * COLS
    rows = views // 2
    return [
        pltpu.VMEM((rows, size, width), jnp.float32),
        pltpu.VMEM((rows, size, width), jnp.float32),
        pltpu.VMEM((rows, size, width), jnp.float32),
        pltpu.VMEM((rows - 1, size, width), jnp.float32),
        pltpu.VMEM((2, size, COLS), jnp.float32),
        pltpu.VMEM((2, size, COLS), jnp.float32),
        pltpu.VMEM((2, pixels), jnp.float32),
        pltpu.VMEM((views - 1, 2, pixels), jnp.float32),
        pltpu.SemaphoreType.DMA((rows,)),
        pltpu.SemaphoreType.DMA((rows,)),
        pltpu.SemaphoreType.DMA((rows - 1,)),
        pltpu.SemaphoreType.DMA((rows - 1,)),
        pltpu.SemaphoreType.DMA((2,)),
        pltpu.SemaphoreType.DMA((2,)),
        pltpu.SemaphoreType.DMA((views - 1,)),
        pltpu.SemaphoreType.DMA((views - 1,)),
    ]


def on_device(ref_feat, src_feat, taps, weights, conv_weight):
    views = lax.axis_size("view")
    tiles = lax.axis_size("tile")
    chans, pixels = ref_feat.shape
    planes = taps.shape[1]
    size = planes // views
    groups = conv_weight.shape[3]
    window = src_feat.shape[3]
    vmem = pl.BlockSpec(memory_space=pltpu.VMEM)
    anywhere = pl.BlockSpec(memory_space=pl.ANY)
    inputs = (taps.reshape(planes), ref_feat, src_feat, weights, conv_weight)
    in_specs = [pl.BlockSpec(memory_space=pltpu.SMEM), anywhere, anywhere, anywhere, vmem]
    outs = (jax.ShapeDtypeStruct((size, pixels), jnp.float32), jax.ShapeDtypeStruct((1, pixels), jnp.float32))
    fetched = [pltpu.VMEM(x.shape, x.dtype) for x in (ref_feat, src_feat, weights)] + [pltpu.SemaphoreType.DMA((3,))]
    local = partial_scratch(chans, window, pixels, planes, groups, size)
    log_prob, depth_map = pl.pallas_call(
        functools.partial(whole_kernel, size, groups, views, tiles),
        out_shape=outs,
        in_specs=in_specs,
        out_specs=(vmem, vmem),
        scratch_shapes=fetched + local + exchange_scratch(views, size, pixels),
        compiler_params=pltpu.CompilerParams(collective_id=0, has_side_effects=True, vmem_limit_bytes=56 * 1024 * 1024),
    )(*inputs)
    return log_prob, depth_map[0]


def solution(mesh):
    placed = (
        P(None, "tile"),
        P("view", "tile", None, None),
        P("view", None, "tile"),
        P("view", None, None, "tile"),
        P(),
    )
    return jax.shard_map(
        on_device,
        mesh=mesh,
        in_specs=placed,
        out_specs=(P("view", "tile"), P("tile")),
        check_vma=False,
    )
```
